256 devices in a mesh: gx: 8 (over z), gy: 8 (over y_lo, x), band: 4 (over y_hi, core).
Axes of the slice: x: 4, y: 4 (y_hi: 2, y_lo: 2; y = y_hi * 2 + y_lo), z: 8, core: 2. Of those that a mesh axis runs over, the one named last changes fastest.
Arguments:
- orbitals: float32 [8, 96, 288, 128], P('band', 'gx', 'gy'), may hold values from -60 to 60
- potential: float32 [96, 288, 128], P('gx', 'gy'), may hold values from -3 to 0
Outputs:
- rotated: float32 [8, 96, 288, 128], P('band', 'gx', 'gy')
- density: float32 [96, 288, 128], P('gx', 'gy')
The draws below stay inside these ranges and needn't reach their ends.
All inputs are finite; a program needn't handle non-finite values.
Results may differ from the reference program's by a relative error of at most 0.00013.
Values sent between devices are 32-bit elements; how exact they have to be, the bound alone decides.
A program may use at most 64 MiB of HBM per device.

```python
import jax
import jax.numpy as jnp
from jax import lax

NB = 8
NZ = 128
NX = 96
NY = 288


def draw_orbitals(key, part):
    key_random, key_scale = jax.random.split(key, 2)
    random_part = jax.random.truncated_normal(key_random, -4.0, 4.0, (NB, NX, NY, NZ), jnp.float32)
    mixed = random_part + 0.6 * jnp.roll(random_part, 1, axis=0)
    scale_draw = jax.random.uniform(key_scale, (NB, 1, 1, 1), jnp.float32)
    band_scale = 0.3 * jnp.exp(jnp.log(10.0) * scale_draw)
    across_x = jnp.arange(NX, dtype=jnp.float32) / NX
    across_y = jnp.arange(NY, dtype=jnp.float32) / NY
    envelope = 0.3 * jnp.exp(jnp.log(10.0) * 0.5 * (across_x[:, None, None] + across_y[None, :, None]))
    return (mixed * band_scale * envelope[None]).astype(jnp.float32)


def level_of(rng, extent, shards, low, high):
    loudness, own = 1.0, jax.random.fold_in(rng, 6)
    for position, shards_of in shards:
        steps = jnp.exp(jax.random.uniform(jax.random.fold_in(own, position), (shards_of,), jnp.float32, low / len(shards), high / len(shards)))
        loudness = loudness * jnp.repeat(steps, extent[position] // shards_of).reshape([-1 if axis == position else 1 for axis in range(len(extent))])
    return loudness


def setup_inputs(seed: int = 0) -> dict:
    seeds = jax.random.split(jax.random.key(seed), 3)
    return {
        "orbitals": draw_orbitals(jax.random.fold_in(seeds[2], 71), 0),
        "potential": jnp.clip(-3.0 + 3.0 * jax.random.uniform(seeds[1], (NX, NY, NZ), jnp.float32) ** level_of(seeds[1], (NX, NY, NZ), ((0, 8), (1, 8)), -0.2, 0.2), -3.0, 0.0),
    }


COEFFS = (-5369.0 / 1800.0, 12.0 / 7.0, -15.0 / 56.0, 10.0 / 189.0, -1.0 / 112.0, 2.0 / 1925.0, -1.0 / 16632.0)
CENTER = 6.25
HALFWIDTH = 4.75
UPPER = 11.0

def product(left, right):
    return jnp.dot(left.astype(jnp.float32), right.astype(jnp.float32), preferred_element_type=jnp.float32, precision=lax.Precision.HIGHEST)

def hamiltonian(field, potential):
    laplace = 3.0 * COEFFS[0] * field
    for dimension in range(3):
        for offset in range(1, 7):
            laplace = laplace + COEFFS[offset] * (jnp.roll(field, offset, dimension) + jnp.roll(field, -offset, dimension))
    return potential * field - 0.5 * laplace

def filter_band(orbital, potential):
    first = (hamiltonian(orbital, potential) - CENTER * orbital) / HALFWIDTH
    second = 2.0 * (hamiltonian(first, potential) - CENTER * first) / HALFWIDTH - orbital
    third = 2.0 * (hamiltonian(second, potential) - CENTER * second) / HALFWIDTH - first
    return (third, hamiltonian(third, potential))

def subspace_rotation(gram_block, ham_block):
    identity = jnp.eye(gram_block.shape[0], dtype=jnp.float32)
    lower = jnp.linalg.cholesky(gram_block)
    inverse = lax.linalg.triangular_solve(lower, identity, left_side=True, lower=True)
    reduced = product(product(inverse, ham_block), inverse.T)
    factor = identity - reduced / UPPER
    return product(inverse.T, factor)

def reference(orbitals, potential):
    filtered, applied = lax.map(lambda single: filter_band(single, potential), orbitals)
    cell_count = NX * NY * NZ
    flattened = filtered.reshape(NB, cell_count)
    applied_flat = applied.reshape(NB, cell_count)
    gram_block = product(flattened, flattened.T) / cell_count
    ham_block = product(applied_flat, flattened.T) / cell_count
    rotation = subspace_rotation(gram_block, ham_block)
    rotated = product(rotation.T, flattened)
    density = jnp.sum(rotated * rotated, axis=0) / NB
    return (rotated.reshape(NB, NX, NY, NZ), density.reshape(NX, NY, NZ))
```

```python
import functools

import jax
import jax.numpy as jnp
from jax import lax
from jax.experimental import pallas as pl
from jax.experimental.pallas import tpu as pltpu
from jax.sharding import PartitionSpec as P

COEFFS = (
    -5369.0 / 1800.0,
    12.0 / 7.0,
    -15.0 / 56.0,
    10.0 / 189.0,
    -1.0 / 112.0,
    2.0 / 1925.0,
    -1.0 / 16632.0,
)
CENTER = 6.25
HALFWIDTH = 4.75
UPPER = 11.0
NB = 8
MESH = pl.DeviceIdType.MESH

LX = 12
LY = 36
ROWS = 2 * LY
HX = 6
HY = 16
PIECES = ((0, 16), (56, 16), (16, 40))
NP = len(PIECES)


def swap_pairs(cells):
    tiles = cells.reshape(-1, 8, 128)
    even = (lax.broadcasted_iota(jnp.int32, tiles.shape, 1) & 1) == 0
    return jnp.where(even, pltpu.roll(tiles, 7, 1), pltpu.roll(tiles, 1, 1)).reshape(cells.shape)


def filter_kernel(
    orb_ref, pot_ref, bands_ref, sums_ref,
    f0, f1, f2, f3, weight, pot, acc, app, swf, swa, gathered, accs, rows_a, rows_b, msg,
    xs, xr, ys, yr, ps, pr, gs, gr, ss, sr, ls,
):
    gx, gy, band = lax.axis_index("gx"), lax.axis_index("gy"), lax.axis_index("band")
    y_lo, x = gy // 4, gy % 4
    y_hi, core = band // 2, band % 2

    load_orb = pltpu.make_async_copy(orb_ref, f0.at[pl.ds(HX, LX), pl.ds(HY, ROWS)], ls.at[0])
    load_pot = pltpu.make_async_copy(pot_ref, pot, ls.at[1])
    load_orb.start()
    load_pot.start()

    group_a = [
        (lax.rem(gx + i, 8), gy, 2 * y_hi + (core if j == 0 else 1 - core))
        for j in range(2) for i in range(8) if i or j
    ]
    group_b = [
        (gx, 4 * (y_lo if a == 0 else 1 - y_lo) + lax.rem(x + i, 4), 2 * (y_hi if b == 0 else 1 - y_hi) + core)
        for b in range(2) for a in range(2) for i in range(4) if a or b or i
    ]
    barrier = pltpu.get_barrier_semaphore()
    for device in group_a + group_b:
        pl.semaphore_signal(barrier, inc=1, device_id=device, device_id_type=MESH)

    x_up, x_down = (lax.rem(gx + 1, 8), gy, band), (lax.rem(gx + 7, 8), gy, band)
    y_up, y_down = (gx, lax.rem(gy + 1, 8), band), (gx, lax.rem(gy + 7, 8), band)
    sibling = (gx, gy, 2 * y_hi + 1 - core)
    partner = (gx, gy, 2 * (1 - y_hi) + core)
    far = 2 * (1 - y_hi) + core
    near = 2 * y_hi + 1 - core
    last = 3 - band

    fields = (f0, f1, f2, f3)

    def remote(src, dst, send, recv, device):
        return pltpu.make_async_remote_copy(
            src_ref=src, dst_ref=dst, send_sem=send, recv_sem=recv, device_id=device, device_id_type=MESH
        )

    def x_copy(step, piece, side):
        field, (first, count) = fields[step], PIECES[piece]
        rows = pl.ds(HY + first, count)
        src, dst, device = ((HX, HX + LX, x_down), (LX, 0, x_up))[side]
        return remote(
            field.at[pl.ds(src, HX), rows], field.at[pl.ds(dst, HX), rows],
            xs.at[step, piece, side], xr.at[step, piece, side], device,
        )

    def y_copy(step, side):
        field = fields[step]
        src, dst, device = ((HY, HY + ROWS, y_down), (ROWS, 0, y_up))[side]
        return remote(
            field.at[pl.ds(HX, LX), pl.ds(src, HY)], field.at[pl.ds(HX, LX), pl.ds(dst, HY)],
            ys.at[step, side], yr.at[step, side], device,
        )

    def band_copy(kind, piece):
        first, count = PIECES[piece]
        mine = f3.at[pl.ds(HX, LX), pl.ds(HY + first, count)]
        rows = pl.ds(first, count)
        if kind == 2:
            src, slot = gathered.at[far, :, rows], far
        else:
            src, slot = mine, band
        return remote(
            src, gathered.at[slot, :, rows], gs.at[kind, piece], gr.at[kind, piece], partner if kind == 0 else sibling
        )

    def send_piece(step, piece):
        sides = (0,) if step == 3 else (0, 1)
        for side in sides:
            x_copy(step, piece, side).start()
        if piece == 0:
            y_copy(step, 0).start()
        if piece == 1 and step < 3:
            y_copy(step, 1).start()
        if step == 3:
            band_copy(0, piece).start()
            band_copy(1, piece).start()

    load_pot.wait()
    load_orb.wait()

    @pl.loop(0, LX)
    def _(layer):
        values = (pot[layer] - (CENTER + 1.5 * COEFFS[0])) * (1.0 / HALFWIDTH)
        weight[layer, pl.ds(0, LY, stride=2), :] = values
        weight[layer, pl.ds(1, LY, stride=2), :] = values

    pl.semaphore_wait(barrier, 30)
    for piece in range(NP):
        send_piece(0, piece)

    for step in range(3):
        field, following = fields[step], fields[step + 1]
        scale = 1.0 if step == 0 else 2.0
        coeffs = [-0.5 * scale * c / HALFWIDTH for c in COEFFS]

        @pl.loop(0, LX)
        def _(layer):
            f = field[HX + layer, pl.ds(HY, ROWS), :]
            total = scale * weight[layer] * f
            if step:
                total = total - fields[step - 1][HX + layer, pl.ds(HY, ROWS), :]
            for k in range(1, 7):
                total = total + coeffs[k] * (pltpu.roll(f, k, 1) + pltpu.roll(f, 128 - k, 1))
            acc[layer] = total

        y_copy(step, 0).wait_recv()
        y_copy(step, 1).wait_recv()

        @pl.loop(0, LX)
        def _(layer):
            total = acc[layer]
            for k in range(1, 7):
                below = field[HX + layer, pl.ds(HY - 2 * k, ROWS), :]
                above = field[HX + layer, pl.ds(HY + 2 * k, ROWS), :]
                total = total + coeffs[k] * (below + above)
            acc[layer] = total

        for piece, (first, count) in enumerate(PIECES):
            x_copy(step, piece, 0).wait_recv()
            x_copy(step, piece, 1).wait_recv()
            rows = pl.ds(HY + first, count)

            @pl.loop(0, LX)
            def _(layer):
                total = acc[layer, pl.ds(first, count), :]
                for k in range(1, 7):
                    total = total + coeffs[k] * (field[HX + layer - k, rows, :] + field[HX + layer + k, rows, :])
                following[HX + layer, rows, :] = total

            send_piece(step + 1, piece)

    coeffs = [-c / HALFWIDTH for c in COEFFS]

    @pl.loop(0, LX)
    def _(layer):
        f = f3[HX + layer, pl.ds(HY, ROWS), :]
        total = weight[layer] * f
        for k in range(1, 7):
            total = total + coeffs[k] * pltpu.roll(f, 128 - k, 1)
        acc[layer] = total
        swf[layer] = swap_pairs(f)

    for piece in (0, 1):
        band_copy(0, piece).wait_recv()
        band_copy(2, piece).start()
    y_copy(3, 0).wait_recv()

    @pl.loop(0, LX)
    def _(layer):
        total = acc[layer]
        for k in range(1, 7):
            total = total + coeffs[k] * f3[HX + layer, pl.ds(HY + 2 * k, ROWS), :]
        acc[layer] = total

    for piece, (first, count) in enumerate(PIECES):
        x_copy(3, piece, 0).wait_recv()

        @pl.loop(0, LX)
        def _(layer):
            total = acc[layer, pl.ds(first, count), :]
            for k in range(1, 7):
                total = total + coeffs[k] * f3[HX + layer + k, pl.ds(HY + first, count), :]
            app[layer, pl.ds(first, count), :] = total
            swa[layer, pl.ds(first, count), :] = swap_pairs(total)

    accs[...] = jnp.zeros_like(accs)

    def products(relative, slot, piece):
        first, count = PIECES[piece]
        rows = pl.ds(first, count)

        def body(layer, carry):
            if slot is None:
                g = f3[HX + layer, pl.ds(HY + first, count), :]
                gathered[band, layer, rows, :] = g
            else:
                g = gathered[slot, layer, rows, :]
            g = g.reshape(-1, 8, 128)
            mine = (f3[HX + layer, pl.ds(HY + first, count), :], swf[layer, rows, :], app[layer, rows, :], swa[layer, rows, :])
            return tuple(c + jnp.sum(m.reshape(-1, 8, 128) * g, axis=0) for c, m in zip(carry, mine))

        start = tuple(accs[pl.ds(8 * (4 * relative + i), 8), :] for i in range(4))
        for i, total in enumerate(lax.fori_loop(0, LX, body, start)):
            accs[pl.ds(8 * (4 * relative + i), 8), :] = total

    for piece in range(NP):
        products(0, None, piece)
    for piece in range(NP):
        band_copy(1, piece).wait_recv()
        products(1, near, piece)
    for piece in (0, 1):
        products(2, far, piece)
    for piece in (0, 1):
        band_copy(2, piece).wait_recv()
        products(3, last, piece)
    band_copy(0, 2).wait_recv()
    band_copy(2, 2).start()
    products(2, far, 2)
    band_copy(2, 2).wait_recv()
    products(3, last, 2)

    store = pltpu.make_async_copy(gathered, bands_ref, ls.at[2])
    store.start()

    highest = lax.Precision.HIGHEST
    by_row = lax.dot_general(
        jnp.ones((8, 128), jnp.float32), accs[...], (((1,), (1,)), ((), ())),
        precision=highest, preferred_element_type=jnp.float32,
    )
    source = lax.broadcasted_iota(jnp.int32, (128, 128), 0)
    target = lax.broadcasted_iota(jnp.int32, (128, 128), 1)
    place = (target == 32 * band + 2 * (source >> 3) + (source & 1)).astype(jnp.float32)
    msg[pl.ds(0, 8), :] = jnp.dot(by_row, place, precision=highest, preferred_element_type=jnp.float32)

    def sum_stage(stage, devices, me, rows):
        rows[pl.ds(me, 1), :] = msg[pl.ds(8 * stage, 1), :]
        copies = [
            remote(msg.at[pl.ds(8 * stage, 1)], rows.at[pl.ds(me, 1)], ss.at[stage, i], sr.at[stage, i], device)
            for i, device in enumerate(devices)
        ]
        for copy in copies:
            copy.start()
        for copy in copies:
            copy.wait_recv()
        return copies

    copies = sum_stage(0, group_a, 2 * gx + core, rows_a)
    total = jnp.sum(rows_a[...], axis=0, keepdims=True)
    msg[pl.ds(8, 8), :] = jnp.broadcast_to(total, (8, 128))
    copies = copies + sum_stage(1, group_b, 4 * (2 * y_hi + y_lo) + x, rows_b)
    total = jnp.sum(rows_b[...], axis=0, keepdims=True)
    sums_ref[...] = jnp.broadcast_to(total, (8, 128))

    for copy in copies:
        copy.wait_send()
    for step in range(4):
        for piece in range(NP):
            for side in (0, 1) if step < 3 else (0,):
                x_copy(step, piece, side).wait_send()
        for side in (0, 1) if step < 3 else (0,):
            y_copy(step, side).wait_send()
    for kind in range(3):
        for piece in range(NP):
            band_copy(kind, piece).wait_send()
    store.wait()


def rotate_kernel(bands_ref, sums_ref, rotated_ref, density_ref, splat, mix, squares):
    band = lax.axis_index("band")
    highest = lax.Precision.HIGHEST
    row = lax.broadcasted_iota(jnp.int32, (128, 128), 0)
    lane = lax.broadcasted_iota(jnp.int32, (128, 128), 1)
    diagonal = jnp.where(row == lane, jnp.broadcast_to(sums_ref[0:1, :], (128, 128)), 0.0)
    splat[...] = jnp.dot(
        diagonal, jnp.ones((128, 128), jnp.float32), precision=highest, preferred_element_type=jnp.float32
    ) * (1.0 / 3538944.0)

    def entry(kind, i, j):
        pair, other = i // 2, j // 2
        lane_of = 32 * pair + 2 * (4 * (pair ^ other) + 2 * kind + (i % 2 != j % 2)) + j % 2
        return jnp.broadcast_to(splat[lane_of : lane_of + 1, :], (8, 128))

    lower, inverse, pivot = {}, {}, {}
    for j in range(NB):
        d = entry(0, j, j)
        for k in range(j):
            d = d - lower[j, k] * lower[j, k]
        pivot[j] = 1.0 / jnp.sqrt(d)
        for i in range(j + 1, NB):
            v = entry(0, i, j)
            for k in range(j):
                v = v - lower[i, k] * lower[j, k]
            lower[i, j] = v * pivot[j]
    for j in range(NB):
        inverse[j, j] = pivot[j]
        for i in range(j + 1, NB):
            v = lower[i, j] * inverse[j, j]
            for k in range(j + 1, i):
                v = v + lower[i, k] * inverse[k, j]
            inverse[i, j] = -v * pivot[i]
    projected = {}
    for i in range(NB):
        for j in range(i + 1):
            projected[i, j] = projected[j, i] = entry(1, i, i) if i == j else 0.5 * (entry(1, i, j) + entry(1, j, i))
    factor = {}
    for i in range(NB):
        half = [sum((inverse[i, k] * projected[k, j] for k in range(1, i + 1)), inverse[i, 0] * projected[0, j]) for j in range(i + 1)]
        for j in range(i + 1):
            v = half[0] * inverse[j, 0]
            for k in range(1, j + 1):
                v = v + half[k] * inverse[j, k]
            v = v * (-HALFWIDTH / UPPER)
            factor[i, j] = factor[j, i] = v + (1.0 - CENTER / UPPER) if i == j else v
    even = (lax.broadcasted_iota(jnp.int32, (8, 128), 0) & 1) == 0
    for k in range(NB // 2):
        columns = {}
        for j in range(NB):
            for b in range(2):
                v = inverse[j, j] * factor[j, 2 * k + b]
                for i in range(j + 1, NB):
                    v = v + inverse[i, j] * factor[i, 2 * k + b]
                columns[j, b] = v
        for q in range(NB // 2):
            mix[8 * k + 2 * q] = jnp.where(even, columns[2 * q, 0], columns[2 * q + 1, 1])
            mix[8 * k + 2 * q + 1] = jnp.where(even, columns[2 * q + 1, 0], columns[2 * q, 1])

    @pl.loop(0, LX)
    def _(layer):
        for tile in range(ROWS // 8):
            rows = pl.ds(8 * tile, 8)
            parts = []
            for q in range(NB // 2):
                g = bands_ref[q, layer, rows, :]
                parts += [g, swap_pairs(g)]
            density = own = None
            for k in range(NB // 2):
                v = mix[8 * k] * parts[0]
                for n in range(1, 8):
                    v = v + mix[8 * k + n] * parts[n]
                density = v * v if density is None else density + v * v
                own = v if own is None else jnp.where(band == k, v, own)
            rotated_ref[layer, rows, :] = own
            squares[rows, :] = density
        density_ref[layer] = (
            squares[pl.ds(0, LY, stride=2), :] + squares[pl.ds(1, LY, stride=2), :]
        ) * (1.0 / NB)


def on_device(orbitals, potential):
    f32 = jnp.float32
    orb = orbitals.transpose(1, 2, 0, 3).reshape(LX, ROWS, 128)
    vmem = functools.partial(pltpu.VMEM, dtype=f32)
    field = vmem((LX + 2 * HX, ROWS + 2 * HY, 128))
    block = vmem((LX, ROWS, 128))
    dma = pltpu.SemaphoreType.DMA
    bands, sums = pl.pallas_call(
        filter_kernel,
        out_shape=(
            jax.ShapeDtypeStruct((4, LX, ROWS, 128), f32),
            jax.ShapeDtypeStruct((8, 128), f32),
        ),
        in_specs=[pl.BlockSpec(memory_space=pl.ANY)] * 2,
        out_specs=(pl.BlockSpec(memory_space=pl.ANY), pl.BlockSpec(memory_space=pltpu.VMEM)),
        scratch_shapes=[
            field, field, field, field, block, vmem((LX, LY, 128)), block, block, block, block,
            vmem((4, LX, ROWS, 128)), vmem((128, 128)), vmem((16, 128)), vmem((16, 128)), vmem((16, 128)),
            dma((4, NP, 2)), dma((4, NP, 2)), dma((4, 2)), dma((4, 2)), dma((1,)), dma((1,)),
            dma((3, NP)), dma((3, NP)), dma((2, 15)), dma((2, 15)), dma((3,)),
        ],
        compiler_params=pltpu.CompilerParams(
            collective_id=0, has_side_effects=True, vmem_limit_bytes=20 * 1024 * 1024
        ),
        name="filter_and_sums",
    )(orb, potential)
    rotated, density = pl.pallas_call(
        rotate_kernel,
        out_shape=(
            jax.ShapeDtypeStruct((LX, ROWS, 128), f32),
            jax.ShapeDtypeStruct((LX, LY, 128), f32),
        ),
        in_specs=[pl.BlockSpec(memory_space=pltpu.VMEM)] * 2,
        out_specs=(pl.BlockSpec(memory_space=pltpu.VMEM),) * 2,
        scratch_shapes=[vmem((128, 128)), vmem((32, 8, 128)), vmem((ROWS, 128))],
        compiler_params=pltpu.CompilerParams(vmem_limit_bytes=20 * 1024 * 1024),
        name="rotate_and_density",
    )(bands, sums)
    return rotated.reshape(LX, LY, 2, 128).transpose(2, 0, 1, 3), density


def solution(mesh):
    return jax.shard_map(
        on_device,
        mesh=mesh,
        in_specs=(P("band", "gx", "gy", None), P("gx", "gy", None)),
        out_specs=(P("band", "gx", "gy", None), P("gx", "gy", None)),
        check_vma=False,
    )
```

```python
import functools

import jax
import jax.numpy as jnp
from jax import lax
from jax.experimental import pallas as pl
from jax.experimental.pallas import tpu as pltpu
from jax.sharding import PartitionSpec as P

COEFFS = (
    -5369.0 / 1800.0,
    12.0 / 7.0,
    -15.0 / 56.0,
    10.0 / 189.0,
    -1.0 / 112.0,
    2.0 / 1925.0,
    -1.0 / 16632.0,
)
CENTER = 6.25
HALFWIDTH = 4.75
UPPER = 11.0
NB = 8
VMEM_BYTES = 60 * 1024 * 1024
MESH = pl.DeviceIdType.MESH

LX = 12
LY = 36
ROWS = 2 * LY
HX = 6
HY = 16
EDGE = 12
PIECES = ((0, 16), (56, 16), (16, 24), (40, 16))
NP = len(PIECES)
PART = 3


def swap_pairs(cells):
    tiles = cells.reshape(-1, 8, 128)
    even = (lax.broadcasted_iota(jnp.int32, tiles.shape, 1) & 1) == 0
    return jnp.where(even, pltpu.roll(tiles, 7, 1), pltpu.roll(tiles, 1, 1)).reshape(cells.shape)


def filter_kernel(
    orb_ref, pot_ref, bands_ref, sums_ref,
    f0, f1, f2, f3, weight, pot, acc, app, swf, swa, gathered, accs, rows_a, rows_b, msg,
    xs, xr, ys, yr, ps, pr, gs, gr, ss, sr, ls,
):
    gx, gy, band = lax.axis_index("gx"), lax.axis_index("gy"), lax.axis_index("band")
    y_lo, x = gy // 4, gy % 4
    y_hi, core = band // 2, band % 2

    load_orb = pltpu.make_async_copy(orb_ref, f0.at[pl.ds(HX, LX), pl.ds(HY, ROWS)], ls.at[0])
    load_pot = pltpu.make_async_copy(pot_ref, pot, ls.at[1])
    load_orb.start()
    load_pot.start()

    group_a = [
        (lax.rem(gx + i, 8), gy, 2 * y_hi + (core if j == 0 else 1 - core))
        for j in range(2) for i in range(8) if i or j
    ]
    group_b = [
        (gx, 4 * (y_lo if a == 0 else 1 - y_lo) + lax.rem(x + i, 4), 2 * (y_hi if b == 0 else 1 - y_hi) + core)
        for b in range(2) for a in range(2) for i in range(4) if a or b or i
    ]
    barrier = pltpu.get_barrier_semaphore()
    x_up, x_down = (lax.rem(gx + 1, 8), gy, band), (lax.rem(gx + 7, 8), gy, band)
    y_up, y_down = (gx, lax.rem(gy + 1, 8), band), (gx, lax.rem(gy + 7, 8), band)
    sibling = (gx, gy, 2 * y_hi + 1 - core)
    partner = (gx, gy, 2 * (1 - y_hi) + core)
    for device in (x_up, x_down, y_up, y_down, sibling, partner):
        pl.semaphore_signal(barrier, inc=1, device_id=device, device_id_type=MESH)
    far = 2 * (1 - y_hi) + core
    near = 2 * y_hi + 1 - core
    last = 3 - band

    fields = (f0, f1, f2, f3)

    def remote(src, dst, send, recv, device):
        return pltpu.make_async_remote_copy(
            src_ref=src, dst_ref=dst, send_sem=send, recv_sem=recv, device_id=device, device_id_type=MESH
        )

    def x_copy(step, piece, side):
        field, (first, count) = fields[step], PIECES[piece]
        rows = pl.ds(HY + first, count)
        src, dst, device = ((HX, HX + LX, x_down), (LX, 0, x_up))[side]
        return remote(
            field.at[pl.ds(src, HX), rows], field.at[pl.ds(dst, HX), rows],
            xs.at[step, piece, side], xr.at[step, piece, side], device,
        )

    def y_copy(step, side):
        field = fields[step]
        src, dst, device = ((HY, HY + ROWS, y_down), (HY + ROWS - EDGE, HY - EDGE, y_up))[side]
        layers = pl.ds(HX + LX // 2 * side, LX // 2) if step == 3 else pl.ds(HX, LX)
        return remote(
            field.at[layers, pl.ds(src, EDGE)], field.at[layers, pl.ds(dst, EDGE)],
            ys.at[step, side], yr.at[step, side], device,
        )

    def band_copy(kind, piece):
        first, count = PIECES[piece]
        mine = f3.at[pl.ds(HX, LX), pl.ds(HY + first, count)]
        rows = pl.ds(first, count)
        if kind == 2:
            src, slot = gathered.at[far, :, rows], far
        else:
            src, slot = mine, band
        return remote(
            src, gathered.at[slot, :, rows], gs.at[kind, piece], gr.at[kind, piece], partner if kind == 0 else sibling
        )

    def send_piece(step, piece):
        sides = (0,) if step == 3 else (0, 1)
        for side in sides:
            x_copy(step, piece, side).start()
        if piece == 0:
            y_copy(step, 0).start()
        if piece == 1:
            y_copy(step, 1).start()
        if step == 3:
            band_copy(0, piece).start()
            band_copy(1, piece).start()

    load_pot.wait()
    load_orb.wait()

    @pl.loop(0, LX)
    def _(layer):
        values = (pot[layer] - (CENTER + 1.5 * COEFFS[0])) * (1.0 / HALFWIDTH)
        weight[layer, pl.ds(0, LY, stride=2), :] = values
        weight[layer, pl.ds(1, LY, stride=2), :] = values

    pl.semaphore_wait(barrier, 6)
    for piece in range(NP):
        send_piece(0, piece)

    for step in range(3):
        field, following = fields[step], fields[step + 1]
        scale = 1.0 if step == 0 else 2.0
        coeffs = [-0.5 * scale * c / HALFWIDTH for c in COEFFS]

        @pl.loop(0, LX)
        def _(layer):
            f = field[HX + layer, pl.ds(HY, ROWS), :]
            total = scale * weight[layer] * f
            if step:
                total = total - fields[step - 1][HX + layer, pl.ds(HY, ROWS), :]
            for k in range(1, 7):
                total = total + coeffs[k] * (pltpu.roll(f, k, 1) + pltpu.roll(f, 128 - k, 1))
            acc[layer] = total

        y_copy(step, 0).wait_recv()
        y_copy(step, 1).wait_recv()

        @pl.loop(0, LX)
        def _(layer):
            total = acc[layer]
            for k in range(1, 7):
                below = field[HX + layer, pl.ds(HY - 2 * k, ROWS), :]
                above = field[HX + layer, pl.ds(HY + 2 * k, ROWS), :]
                total = total + coeffs[k] * (below + above)
            acc[layer] = total

        for piece, (first, count) in enumerate(PIECES):
            x_copy(step, piece, 0).wait_recv()
            x_copy(step, piece, 1).wait_recv()
            rows = pl.ds(HY + first, count)

            @pl.loop(0, LX)
            def _(layer):
                total = acc[layer, pl.ds(first, count), :]
                for k in range(1, 7):
                    total = total + coeffs[k] * (field[HX + layer - k, rows, :] + field[HX + layer + k, rows, :])
                following[HX + layer, rows, :] = total

            send_piece(step + 1, piece)

    coeffs = [-c / HALFWIDTH for c in COEFFS]

    @pl.loop(0, LX)
    def _(layer):
        f = f3[HX + layer, pl.ds(HY, ROWS), :]
        total = weight[layer] * f
        for k in range(1, 7):
            total = total + coeffs[k] * pltpu.roll(f, 128 - k, 1)
        acc[layer] = total
        swf[layer] = swap_pairs(f)

    for side in (0, 1):
        y_copy(3, side).wait_recv()

        @pl.loop(LX // 2 * side, LX // 2 * (side + 1))
        def _(layer):
            total = acc[layer]
            for k in range(1, 7):
                total = total + coeffs[k] * f3[HX + layer, pl.ds(HY + 2 * k * (1 - 2 * side), ROWS), :]
            acc[layer] = total

    for piece in (0, 1):
        band_copy(0, piece).wait_recv()
        band_copy(2, piece).start()

    for piece, (first, count) in enumerate(PIECES):
        x_copy(3, piece, 0).wait_recv()

        @pl.loop(0, LX)
        def _(layer):
            total = acc[layer, pl.ds(first, count), :]
            for k in range(1, 7):
                total = total + coeffs[k] * f3[HX + layer + k, pl.ds(HY + first, count), :]
            app[layer, pl.ds(first, count), :] = total
            swa[layer, pl.ds(first, count), :] = swap_pairs(total)

    accs[...] = jnp.zeros_like(accs)

    def products(relative, slot, piece):
        first, count = PIECES[piece]
        rows = pl.ds(first, count)

        def body(layer, carry):
            if slot is None:
                g = f3[HX + layer, pl.ds(HY + first, count), :]
                gathered[band, layer, rows, :] = g
            else:
                g = gathered[slot, layer, rows, :]
            g = g.reshape(-1, 8, 128)
            mine = (f3[HX + layer, pl.ds(HY + first, count), :], swf[layer, rows, :], app[layer, rows, :], swa[layer, rows, :])
            return tuple(c + jnp.sum(m.reshape(-1, 8, 128) * g, axis=0) for c, m in zip(carry, mine))

        start = tuple(accs[pl.ds(8 * (4 * relative + i), 8), :] for i in range(4))
        for i, total in enumerate(lax.fori_loop(0, LX, body, start)):
            accs[pl.ds(8 * (4 * relative + i), 8), :] = total

    for piece in range(NP):
        products(0, None, piece)
    for piece in range(NP):
        band_copy(1, piece).wait_recv()
        products(1, near, piece)
    for piece in (0, 1):
        products(2, far, piece)
    for piece in range(2, NP):
        band_copy(0, piece).wait_recv()
        band_copy(2, piece).start()
        products(2, far, piece)
    for piece in range(NP):
        band_copy(2, piece).wait_recv()
        products(3, last, piece)

    store = pltpu.make_async_copy(gathered, bands_ref, ls.at[2])
    store.start()

    highest = lax.Precision.HIGHEST
    by_row = lax.dot_general(
        jnp.ones((8, 128), jnp.float32), accs[...], (((1,), (1,)), ((), ())),
        precision=highest, preferred_element_type=jnp.float32,
    )
    source = lax.broadcasted_iota(jnp.int32, (128, 128), 0)
    target = lax.broadcasted_iota(jnp.int32, (128, 128), 1)
    place = (target == 32 * band + 2 * (source >> 3) + (source & 1)).astype(jnp.float32)
    msg[pl.ds(0, 8), :] = jnp.dot(by_row, place, precision=highest, preferred_element_type=jnp.float32)

    def sum_stage(stage, devices, me, rows):
        rows[pl.ds(me, 1), :] = msg[pl.ds(8 * stage, 1), :]
        copies = [
            remote(msg.at[pl.ds(8 * stage, 1)], rows.at[pl.ds(me, 1)], ss.at[stage, i], sr.at[stage, i], device)
            for i, device in enumerate(devices)
        ]
        for copy in copies:
            copy.start()
        for copy in copies:
            copy.wait_recv()
        return copies

    copies = sum_stage(0, group_a, 2 * gx + core, rows_a)
    total = jnp.sum(rows_a[...], axis=0, keepdims=True)
    msg[pl.ds(8, 8), :] = jnp.broadcast_to(total, (8, 128))
    copies = copies + sum_stage(1, group_b, 4 * (2 * y_hi + y_lo) + x, rows_b)
    total = jnp.sum(rows_b[...], axis=0, keepdims=True)
    sums_ref[...] = jnp.broadcast_to(total, (8, 128))

    for copy in copies:
        copy.wait_send()
    for step in range(4):
        for piece in range(NP):
            for side in (0, 1) if step < 3 else (0,):
                x_copy(step, piece, side).wait_send()
        for side in (0, 1):
            y_copy(step, side).wait_send()
    for kind in range(3):
        for piece in range(NP):
            band_copy(kind, piece).wait_send()
    store.wait()


def rotate_kernel(
    bands_ref, sums_ref, rotated_ref, density_ref, bands, sums, rotated, density_out, splat, mix, squares,
    in_sem, out_sem, sums_sem,
):
    band = lax.axis_index("band")
    parts_of = [pl.ds(PART * part, PART) for part in range(LX // PART)]
    loads = [
        pltpu.make_async_copy(bands_ref.at[:, layers], bands.at[:, layers], in_sem.at[part])
        for part, layers in enumerate(parts_of)
    ]
    load_sums = pltpu.make_async_copy(sums_ref, sums, sums_sem.at[0])
    load_sums.start()
    for load in loads:
        load.start()
    load_sums.wait()
    highest = lax.Precision.HIGHEST
    row = lax.broadcasted_iota(jnp.int32, (128, 128), 0)
    lane = lax.broadcasted_iota(jnp.int32, (128, 128), 1)
    diagonal = jnp.where(row == lane, jnp.broadcast_to(sums[0:1, :], (128, 128)), 0.0)
    splat[...] = jnp.dot(
        diagonal, jnp.ones((128, 128), jnp.float32), precision=highest, preferred_element_type=jnp.float32
    ) * (1.0 / 3538944.0)

    def entry(kind, i, j):
        pair, other = i // 2, j // 2
        lane_of = 32 * pair + 2 * (4 * (pair ^ other) + 2 * kind + (i % 2 != j % 2)) + j % 2
        return jnp.broadcast_to(splat[lane_of : lane_of + 1, :], (8, 128))

    lower, inverse, pivot = {}, {}, {}
    for j in range(NB):
        d = entry(0, j, j)
        for k in range(j):
            d = d - lower[j, k] * lower[j, k]
        pivot[j] = 1.0 / jnp.sqrt(d)
        for i in range(j + 1, NB):
            v = entry(0, i, j)
            for k in range(j):
                v = v - lower[i, k] * lower[j, k]
            lower[i, j] = v * pivot[j]
    for j in range(NB):
        inverse[j, j] = pivot[j]
        for i in range(j + 1, NB):
            v = lower[i, j] * inverse[j, j]
            for k in range(j + 1, i):
                v = v + lower[i, k] * inverse[k, j]
            inverse[i, j] = -v * pivot[i]
    projected = {}
    for i in range(NB):
        for j in range(i + 1):
            projected[i, j] = projected[j, i] = entry(1, i, i) if i == j else 0.5 * (entry(1, i, j) + entry(1, j, i))
    factor = {}
    for i in range(NB):
        half = [sum((inverse[i, k] * projected[k, j] for k in range(1, i + 1)), inverse[i, 0] * projected[0, j]) for j in range(i + 1)]
        for j in range(i + 1):
            v = half[0] * inverse[j, 0]
            for k in range(1, j + 1):
                v = v + half[k] * inverse[j, k]
            v = v * (-HALFWIDTH / UPPER)
            factor[i, j] = factor[j, i] = v + (1.0 - CENTER / UPPER) if i == j else v
    even = (lax.broadcasted_iota(jnp.int32, (8, 128), 0) & 1) == 0
    for k in range(NB // 2):
        columns = {}
        for j in range(NB):
            for b in range(2):
                v = inverse[j, j] * factor[j, 2 * k + b]
                for i in range(j + 1, NB):
                    v = v + inverse[i, j] * factor[i, 2 * k + b]
                columns[j, b] = v
        for q in range(NB // 2):
            mix[8 * k + 2 * q] = jnp.where(even, columns[2 * q, 0], columns[2 * q + 1, 1])
            mix[8 * k + 2 * q + 1] = jnp.where(even, columns[2 * q + 1, 0], columns[2 * q, 1])

    stores = []
    for part, layers in enumerate(parts_of):
        loads[part].wait()

        @pl.loop(PART * part, PART * (part + 1))
        def _(layer):
            for tile in range(ROWS // 8):
                rows = pl.ds(8 * tile, 8)
                parts = []
                for q in range(NB // 2):
                    g = bands[q, layer, rows, :]
                    parts += [g, swap_pairs(g)]
                density = own = None
                for k in range(NB // 2):
                    v = mix[8 * k] * parts[0]
                    for n in range(1, 8):
                        v = v + mix[8 * k + n] * parts[n]
                    density = v * v if density is None else density + v * v
                    own = v if own is None else jnp.where(band == k, v, own)
                rotated[layer, rows, :] = own
                squares[rows, :] = density
            density_out[layer] = (
                squares[pl.ds(0, LY, stride=2), :] + squares[pl.ds(1, LY, stride=2), :]
            ) * (1.0 / NB)

        for i, (src, dst) in enumerate(((rotated, rotated_ref), (density_out, density_ref))):
            store = pltpu.make_async_copy(src.at[layers], dst.at[layers], out_sem.at[i, part])
            store.start()
            stores.append(store)
    for store in stores:
        store.wait()


def on_device(orbitals, potential):
    f32 = jnp.float32
    orb = orbitals.transpose(1, 2, 0, 3).reshape(LX, ROWS, 128)
    vmem = functools.partial(pltpu.VMEM, dtype=f32)
    field = vmem((LX + 2 * HX, ROWS + 2 * HY, 128))
    block = vmem((LX, ROWS, 128))
    dma = pltpu.SemaphoreType.DMA
    bands, sums = pl.pallas_call(
        filter_kernel,
        out_shape=(
            jax.ShapeDtypeStruct((4, LX, ROWS, 128), f32),
            jax.ShapeDtypeStruct((8, 128), f32),
        ),
        in_specs=[pl.BlockSpec(memory_space=pl.ANY)] * 2,
        out_specs=(pl.BlockSpec(memory_space=pl.ANY), pl.BlockSpec(memory_space=pltpu.VMEM)),
        scratch_shapes=[
            field, field, field, field, block, vmem((LX, LY, 128)), block, block, block, block,
            vmem((4, LX, ROWS, 128)), vmem((128, 128)), vmem((16, 128)), vmem((16, 128)), vmem((16, 128)),
            dma((4, NP, 2)), dma((4, NP, 2)), dma((4, 2)), dma((4, 2)), dma((1,)), dma((1,)),
            dma((3, NP)), dma((3, NP)), dma((2, 15)), dma((2, 15)), dma((3,)),
        ],
        compiler_params=pltpu.CompilerParams(
            collective_id=0, has_side_effects=True, vmem_limit_bytes=VMEM_BYTES
        ),
        name="filter_and_sums",
    )(orb, potential)
    rotated, density = pl.pallas_call(
        rotate_kernel,
        out_shape=(
            jax.ShapeDtypeStruct((LX, ROWS, 128), f32),
            jax.ShapeDtypeStruct((LX, LY, 128), f32),
        ),
        in_specs=[pl.BlockSpec(memory_space=pl.ANY)] * 2,
        out_specs=(pl.BlockSpec(memory_space=pl.ANY),) * 2,
        scratch_shapes=[
            vmem((4, LX, ROWS, 128)), vmem((8, 128)), block, vmem((LX, LY, 128)),
            vmem((128, 128)), vmem((32, 8, 128)), vmem((ROWS, 128)),
            dma((LX // PART,)), dma((2, LX // PART)), dma((1,)),
        ],
        compiler_params=pltpu.CompilerParams(vmem_limit_bytes=VMEM_BYTES),
        name="rotate_and_density",
    )(bands, sums)
    return rotated.reshape(LX, LY, 2, 128).transpose(2, 0, 1, 3), density


def solution(mesh):
    return jax.shard_map(
        on_device,
        mesh=mesh,
        in_specs=(P("band", "gx", "gy", None), P("gx", "gy", None)),
        out_specs=(P("band", "gx", "gy", None), P("gx", "gy", None)),
        check_vma=False,
    )
```

```python
import functools

import jax
import jax.numpy as jnp
from jax import lax
from jax.experimental import pallas as pl
from jax.experimental.pallas import tpu as pltpu
from jax.sharding import PartitionSpec as P

COEFFS = (
    -5369.0 / 1800.0,
    12.0 / 7.0,
    -15.0 / 56.0,
    10.0 / 189.0,
    -1.0 / 112.0,
    2.0 / 1925.0,
    -1.0 / 16632.0,
)
CENTER = 6.25
HALFWIDTH = 4.75
UPPER = 11.0
NB = 8
VMEM_BYTES = 56_400_000
MESH = pl.DeviceIdType.MESH

LX = 12
LY = 36
ROWS = 2 * LY
HX = 6
HY = 16
EDGE = 12
PIECES = ((0, 16), (56, 16), (16, 24), (40, 16))
NP = len(PIECES)
PART = 3


def swap_pairs(cells):
    tiles = cells.reshape(-1, 8, 128)
    even = (lax.broadcasted_iota(jnp.int32, tiles.shape, 1) & 1) == 0
    return jnp.where(even, pltpu.roll(tiles, 7, 1), pltpu.roll(tiles, 1, 1)).reshape(cells.shape)


def filter_kernel(
    orb_ref, pot_ref, bands_ref, sums_ref,
    f0, f1, f2, f3, weight, pot, acc, zmat, app, swf, swa, near_app, near_swf, near_swa, gathered, accs, rows_a, rows_b, msg,
    xs, xr, ys, yr, ps, pr, gs, gr, ss, sr, ls,
):
    gx, gy, band = lax.axis_index("gx"), lax.axis_index("gy"), lax.axis_index("band")
    y_lo, x = gy // 4, gy % 4
    y_hi, core = band // 2, band % 2

    load_orb = pltpu.make_async_copy(orb_ref, f0.at[pl.ds(HX, LX), pl.ds(HY, ROWS)], ls.at[0])
    load_pot = pltpu.make_async_copy(pot_ref, pot, ls.at[1])
    load_orb.start()
    load_pot.start()

    group_a = [
        (lax.rem(gx + i, 8), gy, 2 * y_hi + (core if j == 0 else 1 - core))
        for j in range(2) for i in range(8) if i or j
    ]
    group_b = [
        (gx, 4 * (y_lo if a == 0 else 1 - y_lo) + lax.rem(x + i, 4), 2 * (y_hi if b == 0 else 1 - y_hi) + core)
        for b in range(2) for a in range(2) for i in range(4) if a or b or i
    ]
    barrier = pltpu.get_barrier_semaphore()
    x_up, x_down = (lax.rem(gx + 1, 8), gy, band), (lax.rem(gx + 7, 8), gy, band)
    y_up, y_down = (gx, lax.rem(gy + 1, 8), band), (gx, lax.rem(gy + 7, 8), band)
    sibling = (gx, gy, 2 * y_hi + 1 - core)
    partner = (gx, gy, 2 * (1 - y_hi) + core)
    for device in (x_up, x_down, y_up, y_down, sibling, partner):
        pl.semaphore_signal(barrier, inc=1, device_id=device, device_id_type=MESH)
    far = 2 * (1 - y_hi) + core
    near = 2 * y_hi + 1 - core
    last = 3 - band

    fields = (f0, f1, f2, f3)

    def remote(src, dst, send, recv, device):
        return pltpu.make_async_remote_copy(
            src_ref=src, dst_ref=dst, send_sem=send, recv_sem=recv, device_id=device, device_id_type=MESH
        )

    def x_copy(step, piece, side):
        field, (first, count) = fields[step], PIECES[piece]
        rows = pl.ds(HY + first, count)
        src, dst, device = ((HX, HX + LX, x_down), (LX, 0, x_up))[side]
        return remote(
            field.at[pl.ds(src, HX), rows], field.at[pl.ds(dst, HX), rows],
            xs.at[step, piece, side], xr.at[step, piece, side], device,
        )

    def y_copy(step, side):
        field = fields[step]
        src, dst, device = ((HY, HY + ROWS, y_down), (HY + ROWS - EDGE, HY - EDGE, y_up))[side]
        layers = pl.ds(HX + LX // 2 * side, LX // 2) if step == 3 else pl.ds(HX, LX)
        return remote(
            field.at[layers, pl.ds(src, EDGE)], field.at[layers, pl.ds(dst, EDGE)],
            ys.at[step, side], yr.at[step, side], device,
        )

    def band_copy(kind, piece):
        first, count = PIECES[piece]
        rows = pl.ds(first, count)
        if kind == 3:
            src, dst = app.at[:, rows], near_app.at[:, rows]
        elif kind == 2:
            src = dst = gathered.at[far, :, rows]
        else:
            src, dst = f3.at[pl.ds(HX, LX), pl.ds(HY + first, count)], gathered.at[band, :, rows]
        return remote(src, dst, gs.at[kind, piece], gr.at[kind, piece], partner if kind == 0 else sibling)

    def send_piece(step, piece):
        sides = (0,) if step == 3 else (0, 1)
        for side in sides:
            x_copy(step, piece, side).start()
        if piece == 0:
            y_copy(step, 0).start()
        if piece == 1:
            y_copy(step, 1).start()
        if step == 3:
            band_copy(0, piece).start()
            band_copy(1, piece).start()

    offset = (lax.broadcasted_iota(jnp.int32, (128, 128), 0) - lax.broadcasted_iota(jnp.int32, (128, 128), 1)) & 127
    for kind in (0, 1):
        matrix = jnp.zeros((128, 128), jnp.float32)
        for k in range(1, 7):
            hit = (offset == k) if kind else (offset == k) | (offset == 128 - k)
            matrix = jnp.where(hit, -(0.5 + 0.5 * kind) * COEFFS[k] / HALFWIDTH, matrix)
        zmat[kind] = matrix

    def local_terms(step, first, count):
        rows = pl.ds(HY + first, count)
        f = fields[step][pl.ds(HX, LX), rows, :]
        along = jnp.dot(
            f.reshape(-1, 128), zmat[step // 3], precision=lax.Precision.HIGHEST, preferred_element_type=jnp.float32
        )
        total = weight[:, pl.ds(first, count), :] * f + along.reshape(f.shape)
        if step in (1, 2):
            total = 2.0 * total - fields[step - 1][pl.ds(HX, LX), rows, :]
        acc[step % 2, :, pl.ds(first, count), :] = total

    load_pot.wait()
    load_orb.wait()

    @pl.loop(0, LX)
    def _(layer):
        values = (pot[layer] - (CENTER + 1.5 * COEFFS[0])) * (1.0 / HALFWIDTH)
        weight[layer, pl.ds(0, LY, stride=2), :] = values
        weight[layer, pl.ds(1, LY, stride=2), :] = values

    local_terms(0, 0, ROWS)
    pl.semaphore_wait(barrier, 6)
    for piece in range(NP):
        send_piece(0, piece)

    for step in range(3):
        field, following = fields[step], fields[step + 1]
        scale = 1.0 if step == 0 else 2.0
        coeffs = [-0.5 * scale * c / HALFWIDTH for c in COEFFS]

        y_copy(step, 0).wait_recv()
        y_copy(step, 1).wait_recv()

        @pl.loop(0, LX)
        def _(layer):
            total = acc[step % 2, layer]
            for k in range(1, 7):
                below = field[HX + layer, pl.ds(HY - 2 * k, ROWS), :]
                above = field[HX + layer, pl.ds(HY + 2 * k, ROWS), :]
                total = total + coeffs[k] * (below + above)
            acc[step % 2, layer] = total

        for piece, (first, count) in enumerate(PIECES):
            x_copy(step, piece, 0).wait_recv()
            x_copy(step, piece, 1).wait_recv()
            rows = pl.ds(HY + first, count)

            @pl.loop(0, LX)
            def _(layer):
                total = acc[step % 2, layer, pl.ds(first, count), :]
                for k in range(1, 7):
                    total = total + coeffs[k] * (field[HX + layer - k, rows, :] + field[HX + layer + k, rows, :])
                following[HX + layer, rows, :] = total

            send_piece(step + 1, piece)
            local_terms(step + 1, first, count)

    coeffs = [-c / HALFWIDTH for c in COEFFS]

    @pl.loop(0, LX)
    def _(layer):
        swf[layer] = swap_pairs(f3[HX + layer, pl.ds(HY, ROWS), :])

    for side in (0, 1):
        y_copy(3, side).wait_recv()

        @pl.loop(LX // 2 * side, LX // 2 * (side + 1))
        def _(layer):
            total = acc[1, layer]
            for k in range(1, 7):
                total = total + coeffs[k] * f3[HX + layer, pl.ds(HY + 2 * k * (1 - 2 * side), ROWS), :]
            acc[1, layer] = total


    for piece, (first, count) in enumerate(PIECES):
        x_copy(3, piece, 0).wait_recv()

        @pl.loop(0, LX)
        def _(layer):
            total = acc[1, layer, pl.ds(first, count), :]
            for k in range(1, 7):
                total = total + coeffs[k] * f3[HX + layer + k, pl.ds(HY + first, count), :]
            app[layer, pl.ds(first, count), :] = total
            swa[layer, pl.ds(first, count), :] = swap_pairs(total)

        band_copy(3, piece).start()

    accs[...] = jnp.zeros_like(accs)

    def products(relative, slot, piece):
        first, count = PIECES[piece]
        rows = pl.ds(first, count)

        def body(layer, carry):
            if slot is None:
                g = f3[HX + layer, pl.ds(HY + first, count), :]
                gathered[band, layer, rows, :] = g
            else:
                g = gathered[slot, layer, rows, :]
            g = g.reshape(-1, 8, 128)
            if relative == 3:
                mine = (gathered[near, layer, rows, :], near_swf[layer, rows, :], near_app[layer, rows, :], near_swa[layer, rows, :])
            else:
                mine = (f3[HX + layer, pl.ds(HY + first, count), :], swf[layer, rows, :], app[layer, rows, :], swa[layer, rows, :])
            return tuple(c + jnp.sum(m.reshape(-1, 8, 128) * g, axis=0) for c, m in zip(carry, mine))

        start = tuple(accs[pl.ds(8 * (4 * relative + i), 8), :] for i in range(4))
        for i, total in enumerate(lax.fori_loop(0, LX, body, start)):
            accs[pl.ds(8 * (4 * relative + i), 8), :] = total

    for piece in range(NP):
        products(0, None, piece)
    for piece in range(NP):
        band_copy(1, piece).wait_recv()
        products(1, near, piece)
    for piece in range(NP):
        band_copy(3, piece).wait_recv()

    @pl.loop(0, LX)
    def _(layer):
        near_swf[layer] = swap_pairs(gathered[near, layer])
        near_swa[layer] = swap_pairs(near_app[layer])

    for piece in range(NP):
        band_copy(0, piece).wait_recv()
        products(2, far, piece)
        products(3, far, piece)

    def store(slot, sem):
        return pltpu.make_async_copy(gathered.at[slot], bands_ref.at[slot], ls.at[sem])

    highest = lax.Precision.HIGHEST
    by_row = lax.dot_general(
        jnp.ones((8, 128), jnp.float32), accs[...], (((1,), (1,)), ((), ())),
        precision=highest, preferred_element_type=jnp.float32,
    )
    source = lax.broadcasted_iota(jnp.int32, (128, 128), 0)
    target = lax.broadcasted_iota(jnp.int32, (128, 128), 1)
    owner = jnp.where(source < 96, band, near)
    place = (target == 32 * owner + 2 * (source >> 3) + (source & 1)).astype(jnp.float32)
    msg[pl.ds(0, 8), :] = jnp.dot(by_row, place, precision=highest, preferred_element_type=jnp.float32)

    def hand_on():
        for piece in range(NP):
            band_copy(2, piece).start()
        store(band, 2).start()
        store(near, 3).start()
        store(far, 4).start()

    def sum_stage(stage, devices, me, rows, meanwhile):
        rows[pl.ds(me, 1), :] = msg[pl.ds(8 * stage, 1), :]
        copies = [
            remote(msg.at[pl.ds(8 * stage, 1)], rows.at[pl.ds(me, 1)], ss.at[stage, i], sr.at[stage, i], device)
            for i, device in enumerate(devices)
        ]
        for copy in copies:
            copy.start()
        meanwhile()
        for copy in copies:
            copy.wait_recv()
        return copies

    copies = sum_stage(0, group_a, 2 * gx + core, rows_a, hand_on)
    total = jnp.sum(rows_a[...], axis=0, keepdims=True)
    msg[pl.ds(8, 8), :] = jnp.broadcast_to(total, (8, 128))

    def take_last():
        for piece in range(NP):
            band_copy(2, piece).wait_recv()
        store(last, 5).start()

    copies = copies + sum_stage(1, group_b, 4 * (2 * y_hi + y_lo) + x, rows_b, take_last)
    total = jnp.sum(rows_b[...], axis=0, keepdims=True)
    sums_ref[...] = jnp.broadcast_to(total, (8, 128))

    for copy in copies:
        copy.wait_send()
    for step in range(4):
        for piece in range(NP):
            for side in (0, 1) if step < 3 else (0,):
                x_copy(step, piece, side).wait_send()
        for side in (0, 1):
            y_copy(step, side).wait_send()
    for kind in range(4):
        for piece in range(NP):
            band_copy(kind, piece).wait_send()
    for slot, sem in ((band, 2), (near, 3), (far, 4), (last, 5)):
        store(slot, sem).wait()


def rotate_kernel(
    bands_ref, sums_ref, rotated_ref, density_ref, bands, rotated, density_out, splat, mix, squares, in_sem, out_sem
):
    band = lax.axis_index("band")
    parts_of = [pl.ds(PART * part, PART) for part in range(LX // PART)]
    loads = [
        pltpu.make_async_copy(bands_ref.at[:, layers], bands.at[:, layers], in_sem.at[part])
        for part, layers in enumerate(parts_of)
    ]
    for load in loads:
        load.start()
    highest = lax.Precision.HIGHEST
    row = lax.broadcasted_iota(jnp.int32, (128, 128), 0)
    lane = lax.broadcasted_iota(jnp.int32, (128, 128), 1)
    diagonal = jnp.where(row == lane, jnp.broadcast_to(sums_ref[0:1, :], (128, 128)), 0.0)
    splat[...] = jnp.dot(
        diagonal, jnp.ones((128, 128), jnp.float32), precision=highest, preferred_element_type=jnp.float32
    ) * (1.0 / 3538944.0)

    def entry(kind, i, j):
        pair, other = i // 2, j // 2
        lane_of = 32 * pair + 2 * (4 * (pair ^ other) + 2 * kind + (i % 2 != j % 2)) + j % 2
        return jnp.broadcast_to(splat[lane_of : lane_of + 1, :], (8, 128))

    lower, inverse, pivot = {}, {}, {}
    for j in range(NB):
        d = entry(0, j, j)
        for k in range(j):
            d = d - lower[j, k] * lower[j, k]
        pivot[j] = 1.0 / jnp.sqrt(d)
        for i in range(j + 1, NB):
            v = entry(0, i, j)
            for k in range(j):
                v = v - lower[i, k] * lower[j, k]
            lower[i, j] = v * pivot[j]
    for j in range(NB):
        inverse[j, j] = pivot[j]
        for i in range(j + 1, NB):
            v = lower[i, j] * inverse[j, j]
            for k in range(j + 1, i):
                v = v + lower[i, k] * inverse[k, j]
            inverse[i, j] = -v * pivot[i]
    projected = {}
    for i in range(NB):
        for j in range(i + 1):
            projected[i, j] = projected[j, i] = entry(1, i, i) if i == j else 0.5 * (entry(1, i, j) + entry(1, j, i))
    factor = {}
    for i in range(NB):
        half = [sum((inverse[i, k] * projected[k, j] for k in range(1, i + 1)), inverse[i, 0] * projected[0, j]) for j in range(i + 1)]
        for j in range(i + 1):
            v = half[0] * inverse[j, 0]
            for k in range(1, j + 1):
                v = v + half[k] * inverse[j, k]
            v = v * (-HALFWIDTH / UPPER)
            factor[i, j] = factor[j, i] = v + (1.0 - CENTER / UPPER) if i == j else v
    even = (lax.broadcasted_iota(jnp.int32, (8, 128), 0) & 1) == 0
    for k in range(NB // 2):
        columns = {}
        for j in range(NB):
            for b in range(2):
                v = inverse[j, j] * factor[j, 2 * k + b]
                for i in range(j + 1, NB):
                    v = v + inverse[i, j] * factor[i, 2 * k + b]
                columns[j, b] = v
        for q in range(NB // 2):
            mix[8 * k + 2 * q] = jnp.where(even, columns[2 * q, 0], columns[2 * q + 1, 1])
            mix[8 * k + 2 * q + 1] = jnp.where(even, columns[2 * q + 1, 0], columns[2 * q, 1])

    stores = []
    for part, layers in enumerate(parts_of):
        loads[part].wait()

        @pl.loop(PART * part, PART * (part + 1))
        def _(layer):
            for tile in range(ROWS // 8):
                rows = pl.ds(8 * tile, 8)
                parts = []
                for q in range(NB // 2):
                    g = bands[q, layer, rows, :]
                    parts += [g, swap_pairs(g)]
                density = own = None
                for k in range(NB // 2):
                    v = mix[8 * k] * parts[0]
                    for n in range(1, 8):
                        v = v + mix[8 * k + n] * parts[n]
                    density = v * v if density is None else density + v * v
                    own = v if own is None else jnp.where(band == k, v, own)
                rotated[layer, rows, :] = own
                squares[rows, :] = density
            density_out[layer] = (
                squares[pl.ds(0, LY, stride=2), :] + squares[pl.ds(1, LY, stride=2), :]
            ) * (1.0 / NB)

        for i, (src, dst) in enumerate(((rotated, rotated_ref), (density_out, density_ref))):
            store = pltpu.make_async_copy(src.at[layers], dst.at[layers], out_sem.at[i, part])
            store.start()
            stores.append(store)
    for store in stores:
        store.wait()


def on_device(orbitals, potential):
    f32 = jnp.float32
    orb = orbitals.transpose(1, 2, 0, 3).reshape(LX, ROWS, 128)
    vmem = functools.partial(pltpu.VMEM, dtype=f32)
    field = vmem((LX + 2 * HX, ROWS + 2 * HY, 128))
    block = vmem((LX, ROWS, 128))
    dma = pltpu.SemaphoreType.DMA
    bands, sums = pl.pallas_call(
        filter_kernel,
        out_shape=(
            jax.ShapeDtypeStruct((4, LX, ROWS, 128), f32),
            jax.ShapeDtypeStruct((8, 128), f32),
        ),
        in_specs=[pl.BlockSpec(memory_space=pl.ANY)] * 2,
        out_specs=(pl.BlockSpec(memory_space=pl.ANY), pl.BlockSpec(memory_space=pltpu.VMEM)),
        scratch_shapes=[
            field, field, field, field, block, vmem((LX, LY, 128)), vmem((2, LX, ROWS, 128)), vmem((2, 128, 128)), block, block, block, block, block, block,
            vmem((4, LX, ROWS, 128)), vmem((128, 128)), vmem((16, 128)), vmem((16, 128)), vmem((16, 128)),
            dma((4, NP, 2)), dma((4, NP, 2)), dma((4, 2)), dma((4, 2)), dma((1,)), dma((1,)),
            dma((4, NP)), dma((4, NP)), dma((2, 15)), dma((2, 15)), dma((6,)),
        ],
        compiler_params=pltpu.CompilerParams(
            collective_id=0, has_side_effects=True, vmem_limit_bytes=VMEM_BYTES
        ),
        name="filter_and_sums",
    )(orb, potential)
    rotated, density = pl.pallas_call(
        rotate_kernel,
        out_shape=(
            jax.ShapeDtypeStruct((LX, ROWS, 128), f32),
            jax.ShapeDtypeStruct((LX, LY, 128), f32),
        ),
        in_specs=[pl.BlockSpec(memory_space=pl.ANY), pl.BlockSpec(memory_space=pltpu.VMEM)],
        out_specs=(pl.BlockSpec(memory_space=pl.ANY),) * 2,
        scratch_shapes=[
            vmem((4, LX, ROWS, 128)), block, vmem((LX, LY, 128)),
            vmem((128, 128)), vmem((32, 8, 128)), vmem((ROWS, 128)),
            dma((LX // PART,)), dma((2, LX // PART)),
        ],
        compiler_params=pltpu.CompilerParams(vmem_limit_bytes=VMEM_BYTES),
        name="rotate_and_density",
    )(bands, sums)
    return rotated.reshape(LX, LY, 2, 128).transpose(2, 0, 1, 3), density


def solution(mesh):
    return jax.shard_map(
        on_device,
        mesh=mesh,
        in_specs=(P("band", "gx", "gy", None), P("gx", "gy", None)),
        out_specs=(P("band", "gx", "gy", None), P("gx", "gy", None)),
        check_vma=False,
    )
```

```python
import functools

import jax
import jax.numpy as jnp
from jax import lax
from jax.experimental import pallas as pl
from jax.experimental.pallas import tpu as pltpu
from jax.sharding import PartitionSpec as P

COEFFS = (
    -5369.0 / 1800.0,
    12.0 / 7.0,
    -15.0 / 56.0,
    10.0 / 189.0,
    -1.0 / 112.0,
    2.0 / 1925.0,
    -1.0 / 16632.0,
)
CENTER = 6.25
HALFWIDTH = 4.75
UPPER = 11.0
NB = 8
VMEM_BYTES = 56_400_000
MESH = pl.DeviceIdType.MESH

LX = 12
LY = 36
ROWS = 2 * LY
HX = 6
HY = 16
EDGE = 12
PIECES = ((0, 16), (56, 16), (16, 24), (40, 16))
NP = len(PIECES)
PART = 3


def swap_pairs(cells):
    tiles = cells.reshape(-1, 8, 128)
    even = (lax.broadcasted_iota(jnp.int32, tiles.shape, 1) & 1) == 0
    return jnp.where(even, pltpu.roll(tiles, 7, 1), pltpu.roll(tiles, 1, 1)).reshape(cells.shape)


def filter_kernel(
    orb_ref, pot_ref, bands_ref, sums_ref,
    f0, f1, f2, f3, weight, pot, acc, zmat, app, swf, swa, near_app, near_swf, near_swa, gathered, accs, rows_a, rows_b, msg,
    xs, xr, ys, yr, ps, pr, gs, gr, ss, sr, ls,
):
    gx, gy, band = lax.axis_index("gx"), lax.axis_index("gy"), lax.axis_index("band")
    y_lo, x = gy // 4, gy % 4
    y_hi, core = band // 2, band % 2

    load_orb = pltpu.make_async_copy(orb_ref, f0.at[pl.ds(HX, LX), pl.ds(HY, ROWS)], ls.at[0])
    load_pot = pltpu.make_async_copy(pot_ref, pot, ls.at[1])
    load_orb.start()
    load_pot.start()

    group_a = [
        (lax.rem(gx + i, 8), gy, 2 * y_hi + (core if j == 0 else 1 - core))
        for j in range(2) for i in range(8) if i or j
    ]
    group_b = [
        (gx, 4 * (y_lo if a == 0 else 1 - y_lo) + lax.rem(x + i, 4), 2 * (y_hi if b == 0 else 1 - y_hi) + core)
        for b in range(2) for a in range(2) for i in range(4) if a or b or i
    ]
    barrier = pltpu.get_barrier_semaphore()
    x_up, x_down = (lax.rem(gx + 1, 8), gy, band), (lax.rem(gx + 7, 8), gy, band)
    y_up, y_down = (gx, lax.rem(gy + 1, 8), band), (gx, lax.rem(gy + 7, 8), band)
    sibling = (gx, gy, 2 * y_hi + 1 - core)
    partner = (gx, gy, 2 * (1 - y_hi) + core)
    for device in (x_up, x_down, y_up, y_down, sibling, partner):
        pl.semaphore_signal(barrier, inc=1, device_id=device, device_id_type=MESH)
    far = 2 * (1 - y_hi) + core
    near = 2 * y_hi + 1 - core
    last = 3 - band

    fields = (f0, f1, f2, f3)

    def remote(src, dst, send, recv, device):
        return pltpu.make_async_remote_copy(
            src_ref=src, dst_ref=dst, send_sem=send, recv_sem=recv, device_id=device, device_id_type=MESH
        )

    def x_copy(step, piece, side):
        field, (first, count) = fields[step], PIECES[piece]
        rows = pl.ds(HY + first, count)
        src, dst, device = ((HX, HX + LX, x_down), (LX, 0, x_up))[side]
        return remote(
            field.at[pl.ds(src, HX), rows], field.at[pl.ds(dst, HX), rows],
            xs.at[step, piece, side], xr.at[step, piece, side], device,
        )

    def y_copy(step, side):
        field = fields[step]
        src, dst, device = ((HY, HY + ROWS, y_down), (HY + ROWS - EDGE, HY - EDGE, y_up))[side]
        layers = pl.ds(HX + LX // 2 * side, LX // 2) if step == 3 else pl.ds(HX, LX)
        return remote(
            field.at[layers, pl.ds(src, EDGE)], field.at[layers, pl.ds(dst, EDGE)],
            ys.at[step, side], yr.at[step, side], device,
        )

    def band_copy(kind, piece):
        first, count = PIECES[piece]
        rows = pl.ds(first, count)
        if kind == 3:
            src, dst = app.at[:, rows], near_app.at[:, rows]
        elif kind == 2:
            src = dst = gathered.at[far, :, rows]
        else:
            src, dst = f3.at[pl.ds(HX, LX), pl.ds(HY + first, count)], gathered.at[band, :, rows]
        return remote(src, dst, gs.at[kind, piece], gr.at[kind, piece], partner if kind == 0 else sibling)

    def send_piece(step, piece):
        if step == 3:
            band_copy(0, piece).start()
        sides = (0,) if step == 3 else (0, 1)
        for side in sides:
            x_copy(step, piece, side).start()
        if piece == 0:
            y_copy(step, 0).start()
        if piece == 1:
            y_copy(step, 1).start()

    offset = (lax.broadcasted_iota(jnp.int32, (128, 128), 0) - lax.broadcasted_iota(jnp.int32, (128, 128), 1)) & 127
    for kind in (0, 1):
        matrix = jnp.zeros((128, 128), jnp.float32)
        for k in range(1, 7):
            hit = (offset == k) if kind else (offset == k) | (offset == 128 - k)
            matrix = jnp.where(hit, -(0.5 + 0.5 * kind) * COEFFS[k] / HALFWIDTH, matrix)
        zmat[kind] = matrix

    def local_terms(step, first, count):
        rows = pl.ds(HY + first, count)
        f = fields[step][pl.ds(HX, LX), rows, :]
        along = jnp.dot(
            f.reshape(-1, 128), zmat[step // 3], precision=lax.Precision.HIGHEST, preferred_element_type=jnp.float32
        )
        total = weight[:, pl.ds(first, count), :] * f + along.reshape(f.shape)
        if step in (1, 2):
            total = 2.0 * total - fields[step - 1][pl.ds(HX, LX), rows, :]
        acc[step % 2, :, pl.ds(first, count), :] = total

    load_pot.wait()
    load_orb.wait()

    @pl.loop(0, LX)
    def _(layer):
        values = (pot[layer] - (CENTER + 1.5 * COEFFS[0])) * (1.0 / HALFWIDTH)
        weight[layer, pl.ds(0, LY, stride=2), :] = values
        weight[layer, pl.ds(1, LY, stride=2), :] = values

    local_terms(0, 0, ROWS)
    pl.semaphore_wait(barrier, 6)
    for piece in range(NP):
        send_piece(0, piece)

    for step in range(3):
        field, following = fields[step], fields[step + 1]
        scale = 1.0 if step == 0 else 2.0
        coeffs = [-0.5 * scale * c / HALFWIDTH for c in COEFFS]

        if step:
            local_terms(step, 0, ROWS)
        y_copy(step, 0).wait_recv()
        y_copy(step, 1).wait_recv()

        @pl.loop(0, LX)
        def _(layer):
            total = acc[step % 2, layer]
            for k in range(1, 7):
                below = field[HX + layer, pl.ds(HY - 2 * k, ROWS), :]
                above = field[HX + layer, pl.ds(HY + 2 * k, ROWS), :]
                total = total + coeffs[k] * (below + above)
            acc[step % 2, layer] = total

        for piece, (first, count) in enumerate(PIECES):
            x_copy(step, piece, 0).wait_recv()
            x_copy(step, piece, 1).wait_recv()
            rows = pl.ds(HY + first, count)

            @pl.loop(0, LX)
            def _(layer):
                total = acc[step % 2, layer, pl.ds(first, count), :]
                for k in range(1, 7):
                    total = total + coeffs[k] * (field[HX + layer - k, rows, :] + field[HX + layer + k, rows, :])
                following[HX + layer, rows, :] = total

            send_piece(step + 1, piece)

    local_terms(3, 0, ROWS)
    for piece in range(NP):
        band_copy(1, piece).start()
    coeffs = [-c / HALFWIDTH for c in COEFFS]

    @pl.loop(0, LX)
    def _(layer):
        swf[layer] = swap_pairs(f3[HX + layer, pl.ds(HY, ROWS), :])

    for side in (0, 1):
        y_copy(3, side).wait_recv()

        @pl.loop(LX // 2 * side, LX // 2 * (side + 1))
        def _(layer):
            total = acc[1, layer]
            for k in range(1, 7):
                total = total + coeffs[k] * f3[HX + layer, pl.ds(HY + 2 * k * (1 - 2 * side), ROWS), :]
            acc[1, layer] = total


    for piece, (first, count) in enumerate(PIECES):
        x_copy(3, piece, 0).wait_recv()

        @pl.loop(0, LX)
        def _(layer):
            total = acc[1, layer, pl.ds(first, count), :]
            for k in range(1, 7):
                total = total + coeffs[k] * f3[HX + layer + k, pl.ds(HY + first, count), :]
            app[layer, pl.ds(first, count), :] = total
            swa[layer, pl.ds(first, count), :] = swap_pairs(total)

        band_copy(3, piece).start()

    accs[...] = jnp.zeros_like(accs)

    def products(relative, slot, piece):
        first, count = PIECES[piece]
        rows = pl.ds(first, count)

        def body(layer, carry):
            if slot is None:
                g = f3[HX + layer, pl.ds(HY + first, count), :]
                gathered[band, layer, rows, :] = g
            else:
                g = gathered[slot, layer, rows, :]
            g = g.reshape(-1, 8, 128)
            if relative == 3:
                mine = (gathered[near, layer, rows, :], near_swf[layer, rows, :], near_app[layer, rows, :], near_swa[layer, rows, :])
            else:
                mine = (f3[HX + layer, pl.ds(HY + first, count), :], swf[layer, rows, :], app[layer, rows, :], swa[layer, rows, :])
            return tuple(c + jnp.sum(m.reshape(-1, 8, 128) * g, axis=0) for c, m in zip(carry, mine))

        start = tuple(accs[pl.ds(8 * (4 * relative + i), 8), :] for i in range(4))
        for i, total in enumerate(lax.fori_loop(0, LX, body, start)):
            accs[pl.ds(8 * (4 * relative + i), 8), :] = total

    for piece in range(NP):
        products(0, None, piece)
    for piece in range(NP):
        band_copy(1, piece).wait_recv()
        products(1, near, piece)
    for piece in range(NP):
        band_copy(3, piece).wait_recv()

    @pl.loop(0, LX)
    def _(layer):
        near_swf[layer] = swap_pairs(gathered[near, layer])
        near_swa[layer] = swap_pairs(near_app[layer])

    for piece in range(NP):
        band_copy(0, piece).wait_recv()
        products(2, far, piece)
        products(3, far, piece)

    def store(slot, sem):
        return pltpu.make_async_copy(gathered.at[slot], bands_ref.at[slot], ls.at[sem])

    highest = lax.Precision.HIGHEST
    by_row = lax.dot_general(
        jnp.ones((8, 128), jnp.float32), accs[...], (((1,), (1,)), ((), ())),
        precision=highest, preferred_element_type=jnp.float32,
    )
    source = lax.broadcasted_iota(jnp.int32, (128, 128), 0)
    target = lax.broadcasted_iota(jnp.int32, (128, 128), 1)
    owner = jnp.where(source < 96, band, near)
    place = (target == 32 * owner + 2 * (source >> 3) + (source & 1)).astype(jnp.float32)
    msg[pl.ds(0, 8), :] = jnp.dot(by_row, place, precision=highest, preferred_element_type=jnp.float32)

    def hand_on():
        for piece in range(NP):
            band_copy(2, piece).start()
        store(band, 2).start()
        store(near, 3).start()
        store(far, 4).start()

    def sum_stage(stage, devices, me, rows, meanwhile):
        rows[pl.ds(me, 1), :] = msg[pl.ds(8 * stage, 1), :]
        copies = [
            remote(msg.at[pl.ds(8 * stage, 1)], rows.at[pl.ds(me, 1)], ss.at[stage, i], sr.at[stage, i], device)
            for i, device in enumerate(devices)
        ]
        for copy in copies:
            copy.start()
        meanwhile()
        for copy in copies:
            copy.wait_recv()
        return copies

    copies = sum_stage(0, group_a, 2 * gx + core, rows_a, hand_on)
    total = jnp.sum(rows_a[...], axis=0, keepdims=True)
    msg[pl.ds(8, 8), :] = jnp.broadcast_to(total, (8, 128))

    def take_last():
        for piece in range(NP):
            band_copy(2, piece).wait_recv()
        store(last, 5).start()

    copies = copies + sum_stage(1, group_b, 4 * (2 * y_hi + y_lo) + x, rows_b, take_last)
    total = jnp.sum(rows_b[...], axis=0, keepdims=True)
    sums_ref[...] = jnp.broadcast_to(total, (8, 128))

    for copy in copies:
        copy.wait_send()
    for step in range(4):
        for piece in range(NP):
            for side in (0, 1) if step < 3 else (0,):
                x_copy(step, piece, side).wait_send()
        for side in (0, 1):
            y_copy(step, side).wait_send()
    for kind in range(4):
        for piece in range(NP):
            band_copy(kind, piece).wait_send()
    for slot, sem in ((band, 2), (near, 3), (far, 4), (last, 5)):
        store(slot, sem).wait()


def rotate_kernel(
    bands_ref, sums_ref, rotated_ref, density_ref, bands, rotated, density_out, splat, mix, squares, in_sem, out_sem
):
    band = lax.axis_index("band")
    parts_of = [pl.ds(PART * part, PART) for part in range(LX // PART)]
    loads = [
        pltpu.make_async_copy(bands_ref.at[:, layers], bands.at[:, layers], in_sem.at[part])
        for part, layers in enumerate(parts_of)
    ]
    for load in loads:
        load.start()
    highest = lax.Precision.HIGHEST
    row = lax.broadcasted_iota(jnp.int32, (128, 128), 0)
    lane = lax.broadcasted_iota(jnp.int32, (128, 128), 1)
    diagonal = jnp.where(row == lane, jnp.broadcast_to(sums_ref[0:1, :], (128, 128)), 0.0)
    splat[...] = jnp.dot(
        diagonal, jnp.ones((128, 128), jnp.float32), precision=highest, preferred_element_type=jnp.float32
    ) * (1.0 / 3538944.0)

    def entry(kind, i, j):
        pair, other = i // 2, j // 2
        lane_of = 32 * pair + 2 * (4 * (pair ^ other) + 2 * kind + (i % 2 != j % 2)) + j % 2
        return jnp.broadcast_to(splat[lane_of : lane_of + 1, :], (8, 128))

    lower, inverse, pivot = {}, {}, {}
    for j in range(NB):
        d = entry(0, j, j)
        for k in range(j):
            d = d - lower[j, k] * lower[j, k]
        pivot[j] = 1.0 / jnp.sqrt(d)
        for i in range(j + 1, NB):
            v = entry(0, i, j)
            for k in range(j):
                v = v - lower[i, k] * lower[j, k]
            lower[i, j] = v * pivot[j]
    for j in range(NB):
        inverse[j, j] = pivot[j]
        for i in range(j + 1, NB):
            v = lower[i, j] * inverse[j, j]
            for k in range(j + 1, i):
                v = v + lower[i, k] * inverse[k, j]
            inverse[i, j] = -v * pivot[i]
    projected = {}
    for i in range(NB):
        for j in range(i + 1):
            projected[i, j] = projected[j, i] = entry(1, i, i) if i == j else 0.5 * (entry(1, i, j) + entry(1, j, i))
    factor = {}
    for i in range(NB):
        half = [sum((inverse[i, k] * projected[k, j] for k in range(1, i + 1)), inverse[i, 0] * projected[0, j]) for j in range(i + 1)]
        for j in range(i + 1):
            v = half[0] * inverse[j, 0]
            for k in range(1, j + 1):
                v = v + half[k] * inverse[j, k]
            v = v * (-HALFWIDTH / UPPER)
            factor[i, j] = factor[j, i] = v + (1.0 - CENTER / UPPER) if i == j else v
    even = (lax.broadcasted_iota(jnp.int32, (8, 128), 0) & 1) == 0
    for k in range(NB // 2):
        columns = {}
        for j in range(NB):
            for b in range(2):
                v = inverse[j, j] * factor[j, 2 * k + b]
                for i in range(j + 1, NB):
                    v = v + inverse[i, j] * factor[i, 2 * k + b]
                columns[j, b] = v
        for q in range(NB // 2):
            mix[8 * k + 2 * q] = jnp.where(even, columns[2 * q, 0], columns[2 * q + 1, 1])
            mix[8 * k + 2 * q + 1] = jnp.where(even, columns[2 * q + 1, 0], columns[2 * q, 1])

    stores = []
    for part, layers in enumerate(parts_of):
        loads[part].wait()

        @pl.loop(PART * part, PART * (part + 1))
        def _(layer):
            for tile in range(ROWS // 8):
                rows = pl.ds(8 * tile, 8)
                parts = []
                for q in range(NB // 2):
                    g = bands[q, layer, rows, :]
                    parts += [g, swap_pairs(g)]
                density = own = None
                for k in range(NB // 2):
                    v = mix[8 * k] * parts[0]
                    for n in range(1, 8):
                        v = v + mix[8 * k + n] * parts[n]
                    density = v * v if density is None else density + v * v
                    own = v if own is None else jnp.where(band == k, v, own)
                rotated[layer, rows, :] = own
                squares[rows, :] = density
            density_out[layer] = (
                squares[pl.ds(0, LY, stride=2), :] + squares[pl.ds(1, LY, stride=2), :]
            ) * (1.0 / NB)

        for i, (src, dst) in enumerate(((rotated, rotated_ref), (density_out, density_ref))):
            store = pltpu.make_async_copy(src.at[layers], dst.at[layers], out_sem.at[i, part])
            store.start()
            stores.append(store)
    for store in stores:
        store.wait()


def on_device(orbitals, potential):
    f32 = jnp.float32
    orb = orbitals.transpose(1, 2, 0, 3).reshape(LX, ROWS, 128)
    vmem = functools.partial(pltpu.VMEM, dtype=f32)
    field = vmem((LX + 2 * HX, ROWS + 2 * HY, 128))
    block = vmem((LX, ROWS, 128))
    dma = pltpu.SemaphoreType.DMA
    bands, sums = pl.pallas_call(
        filter_kernel,
        out_shape=(
            jax.ShapeDtypeStruct((4, LX, ROWS, 128), f32),
            jax.ShapeDtypeStruct((8, 128), f32),
        ),
        in_specs=[pl.BlockSpec(memory_space=pl.ANY)] * 2,
        out_specs=(pl.BlockSpec(memory_space=pl.ANY), pl.BlockSpec(memory_space=pltpu.VMEM)),
        scratch_shapes=[
            field, field, field, field, block, vmem((LX, LY, 128)), vmem((2, LX, ROWS, 128)), vmem((2, 128, 128)), block, block, block, block, block, block,
            vmem((4, LX, ROWS, 128)), vmem((128, 128)), vmem((16, 128)), vmem((16, 128)), vmem((16, 128)),
            dma((4, NP, 2)), dma((4, NP, 2)), dma((4, 2)), dma((4, 2)), dma((1,)), dma((1,)),
            dma((4, NP)), dma((4, NP)), dma((2, 15)), dma((2, 15)), dma((6,)),
        ],
        compiler_params=pltpu.CompilerParams(
            collective_id=0, has_side_effects=True, vmem_limit_bytes=VMEM_BYTES
        ),
        name="filter_and_sums",
    )(orb, potential)
    rotated, density = pl.pallas_call(
        rotate_kernel,
        out_shape=(
            jax.ShapeDtypeStruct((LX, ROWS, 128), f32),
            jax.ShapeDtypeStruct((LX, LY, 128), f32),
        ),
        in_specs=[pl.BlockSpec(memory_space=pl.ANY), pl.BlockSpec(memory_space=pltpu.VMEM)],
        out_specs=(pl.BlockSpec(memory_space=pl.ANY),) * 2,
        scratch_shapes=[
            vmem((4, LX, ROWS, 128)), block, vmem((LX, LY, 128)),
            vmem((128, 128)), vmem((32, 8, 128)), vmem((ROWS, 128)),
            dma((LX // PART,)), dma((2, LX // PART)),
        ],
        compiler_params=pltpu.CompilerParams(vmem_limit_bytes=VMEM_BYTES),
        name="rotate_and_density",
    )(bands, sums)
    return rotated.reshape(LX, LY, 2, 128).transpose(2, 0, 1, 3), density


def solution(mesh):
    return jax.shard_map(
        on_device,
        mesh=mesh,
        in_specs=(P("band", "gx", "gy", None), P("gx", "gy", None)),
        out_specs=(P("band", "gx", "gy", None), P("gx", "gy", None)),
        check_vma=False,
    )
```
